256 devices in a mesh: chan: 32 (over x_hi, z, core), freq: 8 (over x_lo, y).
Axes of the slice: x: 4 (x_hi: 2, x_lo: 2; x = x_hi * 2 + x_lo), y: 4, z: 8, core: 2. Of those that a mesh axis runs over, the one named last changes fastest.
Arguments:
- spectra: bfloat16 [2, 2, 2048, 16384], P(None, None, 'freq', 'chan'), may hold values from -6 to 6
- gap: int32 [16384], P('chan'), may hold values 0 or 1
- reach: int32 [128], P('chan'), may hold values from 1 to 8, as said below
- valid: int32 [128, 8], P('chan'), may hold values 0 or 1
Outputs:
- upper: float32 [128, 128, 8, 2, 128], P('freq', 'chan')
- lower: float32 [128, 128, 8, 2, 128], P('freq', 'chan')
The draws below stay inside these ranges and needn't reach their ends.
Inputs may be any that keep to these rules, and one draw needn't show every extreme that they name: reach of some block equals 8 in every draw.
All inputs are finite; a program needn't handle non-finite values. No bound on the sum of `gap` or of `valid` on one device may be relied on, other than what follows from the above.
Results may differ from the reference program's by a relative error of at most 0.0003.
Values may be sent and summed in bfloat16 or wider, within the bound.
A program may use at most 64 MiB of HBM per device.

```python
import math
import jax
import jax.numpy as jnp

CHANNELS = 16384
BLOCK = 128
BINS = 2048
SEGS = 2
KOFF = 8
NBLK = 128


def draw_reach(key, part):
    key = jax.random.fold_in(key, 11)
    first_key, second_key = jax.random.split(key)
    values = jax.random.randint(first_key, (NBLK,), 1, KOFF + 1)
    spot = jax.random.randint(second_key, (), 0, NBLK)
    return jnp.where(jnp.arange(NBLK) == spot, KOFF, values).astype(jnp.int32)


def place_ends(values, own_key, least, high):
    longest = values.shape.index(max(values.shape))
    spots = []
    for shift in (0, 1):
        where = [jax.random.randint(jax.random.fold_in(own_key, axis), (), 0, length) for axis, length in enumerate(values.shape)]
        where[longest] = (where[longest] + shift) % values.shape[longest]
        spots.append(tuple(where))
    return values.at[spots[0]].set(least).at[spots[1]].set(high)


def block_scale(stream_key, extent, cuts, smallest, top_value):
    def one(position, parts):
        steps = jax.random.uniform(jax.random.fold_in(jax.random.fold_in(stream_key, 6), position), (parts,), jnp.float32, smallest / len(cuts), top_value / len(cuts))
        return jnp.repeat(jnp.exp(steps), extent[position] // parts).reshape((-1,) + (1,) * (len(extent) - position - 1))

    loudness = one(*cuts[0])
    for cut in cuts[1:]:
        loudness = loudness * one(*cut)
    return loudness


def bell_draw(rng, dims, scale, bound, cuts=(), kind=jnp.bfloat16):
    result = jax.random.normal(rng, dims, jnp.float32) * scale
    if len(cuts) > 0:
        result = block_scale(rng, dims, cuts, -0.22, 0.18) * result
    return jnp.clip(result, min=-bound, max=bound).astype(kind)


def setup_inputs(seed: int = 0) -> dict:
    key_list = jax.random.split(jax.random.key(seed), 5)
    return {
        "spectra": bell_draw(key_list[0], (2, SEGS, BINS, CHANNELS), 1.0, 6.0, ((2, 8), (3, 32))),
        "gap": place_ends((jax.random.randint(key_list[1], (CHANNELS,), 0, 8) < 7).astype(jnp.int32), jax.random.fold_in(key_list[1], 1), 0, 1),
        "reach": draw_reach(jax.random.fold_in(key_list[4], 71), 0),
        "valid": place_ends((jax.random.randint(key_list[3], (NBLK, KOFF), 0, 4) < 3).astype(jnp.int32), jax.random.fold_in(key_list[3], 1), 0, 1),
    }


def reference(spectra, gap, reach, valid):
    live = gap.astype(jnp.float32)
    data = spectra.astype(jnp.float32) * live
    turned = jnp.stack([data[1], -data[0]])
    depth = 2 * SEGS * BINS
    left = data.reshape(depth, NBLK, BLOCK)
    twin = turned.reshape(depth, NBLK, BLOCK)
    scale = 1.0 / math.sqrt(SEGS * BINS)
    blocks = jnp.arange(NBLK)
    sign = jnp.array([1.0, -1.0], dtype=jnp.float32)
    uppers = []
    lowers = []
    for k in range(KOFF):
        count = NBLK - k
        first = left[:, :count]
        second = left[:, k:]
        second_twin = twin[:, k:]
        real = jnp.einsum('cbi,cbj->ibj', first, second)
        imag = jnp.einsum('cbi,cbj->ibj', first, second_twin)
        pair = jnp.stack([real, imag], axis=2) * scale
        keep = (k < reach) & (valid[:, k] > 0) & (blocks < count)
        keep = keep.astype(jnp.float32)
        pair = jnp.pad(pair, ((0, 0), (0, k), (0, 0), (0, 0)))
        pair = pair * keep[None, :, None, None]
        uppers.append(pair)
        moved = jnp.pad(pair[:, :count], ((0, 0), (k, 0), (0, 0), (0, 0)))
        lowers.append(moved * sign[None, None, :, None])
    upper = jnp.stack(uppers, axis=2)
    lower = jnp.stack(lowers, axis=2)
    return (upper, lower)
```

```python
import math

import jax
import jax.numpy as jnp
from jax import lax
from jax.experimental import pallas as pl
from jax.experimental.pallas import tpu as pltpu
from jax.sharding import PartitionSpec as P

BINS = 2048
SEGS = 2
KOFF = 8
LANE = 128
OWN = 4
PREV = 3
KEEP = 16
HALVES = 2
RING = 4
EXTRA = 8
FULL = 32700.0
MID = 32768
SMALLEST = 1e-33
ON_MESH = pl.DeviceIdType.MESH

GROUPS = (
    ("x", ((0, 1, 3, 0), (1, 2, 4, 0), (2, 3, 5, 0))),
    ("y", ((3, 4, 6, 0),)),
    ("x", ((4, 4, 6, 1),)),
    ("y", ((5, 4, 6, 2),)),
    ("x", ((6, 4, 6, 3),)),
    ("y", ((4, 3, 2, 5), (5, 2, 2, 6), (6, 1, 2, 7))),
    ("x", ((7, 4, 6, 4),)),
)


def group_pairs(group):
    return sum(job[1] for job in group[1])


def packed(re, im):
    top = jnp.max(jnp.maximum(jnp.abs(re), jnp.abs(im)), axis=0, keepdims=True)
    power = jnp.ceil(jnp.log2(jnp.maximum(top, SMALLEST)))
    factor = FULL * jnp.exp2(-power)
    high = (re * factor + (MID + 0.5)).astype(jnp.int32)
    low = (im * factor + (MID + 0.5)).astype(jnp.int32)
    return lax.bitwise_or(lax.shift_left(high, jnp.full_like(high, 16)), low), power.astype(jnp.int32)


def unpacked(word, power):
    step = jnp.exp2(power.astype(jnp.float32)) * (1.0 / FULL)
    high = lax.shift_right_logical(word, jnp.full_like(word, 16)) - MID
    low = lax.bitwise_and(word, jnp.full_like(word, 65535)) - MID
    return high.astype(jnp.float32) * step, low.astype(jnp.float32) * step


def kernel(reach_ref, valid_ref, gap_ref, spectra_ref, upper_ref, lower_ref, *scratch):
    right, left, turned, weights, weights_prev, send_sem, recv_sem = scratch[:7]
    buffers = [scratch[7 + 6 * g : 13 + 6 * g] for g in range(len(GROUPS))]
    depth = spectra_ref.shape[0]
    half = depth // 2
    lanes = lax.axis_size("chan")
    chan = lax.axis_index("chan")
    freq = lax.axis_index("freq")
    x_own = freq // RING
    y_own = lax.rem(freq, RING)
    after = (lax.rem(chan + 1, lanes), freq)
    before = (lax.rem(chan + lanes - 1, lanes), freq)
    across = (chan, (1 - x_own) * RING + y_own)
    around = [(chan, x_own * RING + lax.rem(y_own + step, RING)) for step in range(1, RING)]

    barrier = pltpu.get_barrier_semaphore()
    for peer in [after, before, across] + around:
        pl.semaphore_signal(barrier, inc=1, device_id=peer, device_id_type=ON_MESH)

    count = [0]

    def remote(source, target, peer):
        slot = count[0]
        count[0] = slot + 1
        return pltpu.make_async_remote_copy(
            src_ref=source,
            dst_ref=target,
            send_sem=send_sem.at[slot],
            recv_sem=recv_sem.at[slot],
            device_id=peer,
            device_id_type=ON_MESH,
        )

    for b in range(OWN):
        live = gap_ref[b : b + 1, :].astype(jnp.float32).astype(jnp.bfloat16)
        right[b] = spectra_ref[:, b * LANE : (b + 1) * LANE] * live
    for i in range(OWN):
        for k in range(KOFF):
            keep = (k < reach_ref[i]) & (valid_ref[i, k] > 0) & (chan * OWN + i + k < lanes * OWN)
            value = jnp.where(keep, 1.0 / math.sqrt(SEGS * BINS), 0.0).astype(jnp.float32)
            weights[i * KOFF + k : i * KOFF + k + 1, :] = jnp.full((1, LANE), value, jnp.float32)

    pl.semaphore_wait(barrier, 6)
    send_right = [remote(right.at[b], right.at[OWN + b], before) for b in range(OWN)]
    for copy in send_right:
        copy.start()

    send_left = [remote(left.at[PREV + b], left.at[b - 1], after) for b in range(1, OWN)]
    for b in reversed(range(OWN)):
        for t in range(depth // LANE):
            tile = right[b, t * LANE : (t + 1) * LANE, :]
            turned[:, t * LANE : (t + 1) * LANE] = tile.T
        for hx in range(HALVES):
            for dy in range(RING):
                part = lax.rem(x_own + hx, HALVES) * RING + lax.rem(y_own + dy, RING)
                row = pl.multiple_of(part * KEEP, KEEP)
                to = (hx * RING + dy) * KEEP
                left[PREV + b, to : to + KEEP, :] = turned[pl.ds(row, KEEP), :]
        if b > 0:
            send_left[b - 1].start()
    send_weights = remote(weights, weights_prev, after)
    send_weights.start()

    first, second = [], []
    for (kind, _), (_, s1, r1, s2, r2, _) in zip(GROUPS, buffers):
        one_x = lambda s, r: [remote(s.at[0], r.at[0], across)]
        all_y = lambda s, r: [remote(s.at[d], r.at[d], around[d]) for d in range(RING - 1)]
        first.append(one_x(s1, r1) if kind == "x" else all_y(s1, r1))
        second.append(all_y(s2, r2) if kind == "x" else one_x(s2, r2))

    def put(ref, piece, rows, total, s, re, im):
        word, power = packed(re, im)
        ref[piece, pl.ds(pl.multiple_of(s * rows, rows), rows), :] = word
        ref[piece, pl.ds(total * rows + s, 1), :] = power

    def take(ref, piece, rows, total, s):
        word = ref[piece, pl.ds(pl.multiple_of(s * rows, rows), rows), :]
        return unpacked(word, ref[piece, pl.ds(total * rows + s, 1), :])

    def compute(g):
        kind, jobs = GROUPS[g]
        total = group_pairs(GROUPS[g])
        acc, s1 = buffers[g][0], buffers[g][1]
        side = HALVES * KEEP
        base = 0
        for column, pairs, row, _ in jobs:

            def step(n, carry, column=column, row=row, base=base):
                s = base + n
                a = left[row - n]
                re = jnp.dot(a, right[column], preferred_element_type=jnp.float32)
                im = jnp.dot(a[:, :half], right[column, half:], preferred_element_type=jnp.float32)
                im = im - jnp.dot(a[:, half:], right[column, :half], preferred_element_type=jnp.float32)
                if kind == "x":
                    span = RING * KEEP
                    acc[s, 0] = re[:span]
                    acc[s, 1] = im[:span]
                    put(s1, 0, span, total, s, re[span:], im[span:])
                else:
                    for dy in range(RING):
                        low, high = dy * KEEP, (RING + dy) * KEEP
                        re_part = jnp.concatenate([re[low : low + KEEP], re[high : high + KEEP]], axis=0)
                        im_part = jnp.concatenate([im[low : low + KEEP], im[high : high + KEEP]], axis=0)
                        if dy == 0:
                            acc[s, 0] = re_part
                            acc[s, 1] = im_part
                        else:
                            put(s1, dy - 1, side, total, s, re_part, im_part)
                return carry

            lax.fori_loop(0, pairs, step, 0)
            base += pairs
        for copy in first[g]:
            copy.start()

    def middle(g):
        kind, _ = GROUPS[g]
        total = group_pairs(GROUPS[g])
        acc, _, r1, s2 = buffers[g][:4]
        for copy in first[g]:
            copy.wait_recv()

        def step(s, carry):
            re, im = acc[s, 0], acc[s, 1]
            for piece in range(len(first[g])):
                more_re, more_im = take(r1, piece, re.shape[0], total, s)
                re, im = re + more_re, im + more_im
            acc[s, 0, :KEEP] = re[:KEEP]
            acc[s, 1, :KEEP] = im[:KEEP]
            for piece in range(len(second[g])):
                rows = slice((piece + 1) * KEEP, (piece + 2) * KEEP)
                put(s2, piece, KEEP, total, s, re[rows], im[rows])
            return carry

        lax.fori_loop(0, total, step, 0)
        for copy in second[g]:
            copy.start()

    outgoing = []

    def finish(g):
        _, jobs = GROUPS[g]
        total = group_pairs(GROUPS[g])
        acc, r2, done = buffers[g][0], buffers[g][4], buffers[g][5]
        for copy in second[g]:
            copy.wait_recv()
        s = 0
        for column, pairs, row, offset in jobs:
            start = s
            for n in range(pairs):
                i, k = row - n - PREV, offset + n
                re, im = acc[s, 0, :KEEP], acc[s, 1, :KEEP]
                for piece in range(len(second[g])):
                    more_re, more_im = take(r2, piece, KEEP, total, s)
                    re, im = re + more_re, im + more_im
                at = (i % OWN) * KOFF + k
                scale = (weights if i >= 0 else weights_prev)[at : at + 1, :]
                re, im = re * scale, im * scale
                if i >= 0:
                    upper_ref[at, 0] = re
                    upper_ref[at, 1] = im
                if column < OWN:
                    lower_ref[column * KOFF + k, 0] = re
                    lower_ref[column * KOFF + k, 1] = im
                else:
                    done[s, 0] = re
                    done[s, 1] = im
                if i < 0:
                    outgoing.append(remote(done.at[s], upper_ref.at[at], before))
                s += 1
            if column >= OWN:
                at = (column - OWN) * KOFF + offset
                outgoing.append(remote(done.at[pl.ds(start, pairs)], lower_ref.at[pl.ds(at, pairs)], after))
        return

    started = [0]

    def launch():
        for copy in outgoing[started[0] :]:
            copy.start()
        started[0] = len(outgoing)

    compute(0)
    compute(1)
    send_right[0].wait_recv()
    compute(2)
    middle(0)
    send_right[1].wait_recv()
    compute(3)
    middle(1)
    finish(0)
    send_right[2].wait_recv()
    compute(4)
    middle(2)
    finish(1)
    for copy in send_left:
        copy.wait_recv()
    compute(5)
    middle(3)
    finish(2)
    launch()
    send_right[3].wait_recv()
    compute(6)
    middle(4)
    finish(3)
    launch()
    middle(5)
    finish(4)
    launch()
    middle(6)
    send_weights.wait_recv()
    finish(5)
    launch()
    finish(6)
    launch()
    for copy in outgoing:
        copy.wait_recv()
    for copy in send_right + send_left + [send_weights] + sum(first, []) + sum(second, []) + outgoing:
        copy.wait_send()


def scratch_shapes(depth):
    shapes = [
        pltpu.VMEM((2 * OWN, depth, LANE), jnp.bfloat16),
        pltpu.VMEM((PREV + OWN, LANE, depth), jnp.bfloat16),
        pltpu.VMEM((LANE, depth), jnp.bfloat16),
        pltpu.VMEM((OWN * KOFF, LANE), jnp.float32),
        pltpu.VMEM((OWN * KOFF, LANE), jnp.float32),
        pltpu.SemaphoreType.DMA((64,)),
        pltpu.SemaphoreType.DMA((64,)),
    ]
    for group in GROUPS:
        total = group_pairs(group)
        wide = RING if group[0] == "x" else HALVES
        one = lambda rows: pltpu.VMEM((1, total * rows + EXTRA, LANE), jnp.int32)
        three = lambda rows: pltpu.VMEM((RING - 1, total * rows + EXTRA, LANE), jnp.int32)
        s1 = (one if group[0] == "x" else three)(wide * KEEP)
        s2 = (three if group[0] == "x" else one)(KEEP)
        shapes += [
            pltpu.VMEM((total, 2, wide * KEEP, LANE), jnp.float32),
            s1,
            s1,
            s2,
            s2,
            pltpu.VMEM((total, 2, KEEP, LANE), jnp.float32),
        ]
    return shapes


def shards(spectra, gap, reach, valid):
    depth = spectra.shape[0] * spectra.shape[1] * spectra.shape[2]
    flat = spectra.reshape(depth, spectra.shape[3])
    pairs = OWN * KOFF
    result = jax.ShapeDtypeStruct((pairs, 2, KEEP, LANE), jnp.float32)
    in_vmem = pl.BlockSpec(memory_space=pltpu.VMEM)
    in_smem = pl.BlockSpec(memory_space=pltpu.SMEM)
    upper, lower = pl.pallas_call(
        kernel,
        out_shape=(result, result),
        in_specs=[in_smem, in_smem, in_vmem, in_vmem],
        out_specs=(in_vmem, in_vmem),
        scratch_shapes=scratch_shapes(depth),
        compiler_params=pltpu.CompilerParams(
            collective_id=0, has_side_effects=True, vmem_limit_bytes=40 * 2**20
        ),
        cost_estimate=pl.CostEstimate(flops=4 * pairs * depth * LANE * LANE, bytes_accessed=2**21, transcendentals=0),
        name="spectral_pairs",
    )(reach, valid, gap.reshape(OWN, LANE), flat)
    order = (3, 0, 1, 2, 4)
    sign = jnp.array([1.0, -1.0], dtype=jnp.float32)
    upper = upper.reshape(OWN, KOFF, 2, KEEP, LANE).transpose(order)
    lower = lower.reshape(OWN, KOFF, 2, KEEP, LANE).transpose(order)
    return upper, lower * sign[None, None, None, :, None]


def solution(mesh):
    placed = (P(None, None, "freq", "chan"), P("chan"), P("chan"), P("chan", None))
    return jax.shard_map(
        shards,
        mesh=mesh,
        in_specs=placed,
        out_specs=(P("freq", "chan", None, None, None), P("freq", "chan", None, None, None)),
        check_vma=False,
    )
```

```python
import math

import jax
import jax.numpy as jnp
from jax import lax
from jax.experimental import pallas as pl
from jax.experimental.pallas import tpu as pltpu
from jax.sharding import PartitionSpec as P

BINS = 2048
SEGS = 2
KOFF = 8
LANE = 128
OWN = 4
PREV = 3
KEEP = 16
RING = 4
SHARES = 8
POWERS = 4
FULL = 32700.0
MID = 32768
SMALLEST = 1e-33
ON_MESH = pl.DeviceIdType.MESH

FLIPS = {"x": 4, "b": 2, "a": 1}
OWN_FIRST = ((0, 1, 3, 0), (1, 2, 4, 0), (2, 3, 5, 0))
OWN_LAST = ((3, 4, 6, 0),)
EVEN = (
    (("b", "x", "a"), OWN_FIRST),
    (("a", "b", "x"), OWN_LAST),
    (("b", "a", "x"), ((4, 4, 6, 1),)),
    (("b", "x", "a"), ((5, 4, 6, 2),)),
    (("a", "b", "x"), ((6, 4, 6, 3),)),
    (("b", "a", "x"), ((7, 4, 6, 4),)),
    (("a", "x", "b"), ((4, 1, 2, 5), (5, 1, 2, 6), (6, 1, 2, 7))),
    (("b", "xa"), ((4, 2, 1, 6), (5, 1, 1, 7))),
)
ODD = (
    (("b", "a", "x"), OWN_FIRST),
    (("a", "x", "b"), OWN_LAST),
    (("a", "xb"), ((4, 7, 6, 1),)),
    (("x", "ab"), ((5, 6, 6, 2),)),
    (("a", "xb"), ((6, 5, 6, 3),)),
    (("b", "xa"), ((7, 4, 6, 4),)),
)
EVEN_STEPS = (
    "c0", "c1", "a4", "w", "c2", "a5", "c3", "a6", "c4", "a7", "c5", "p2", "c6", "m1.1", "m0.1", "m4.1",
    "m2.1", "p1", "p0", "c7", "m3.1", "m6.1", "m5.1", "m0.2", "m1.2", "m2.2", "m4.2", "m3.2", "m6.2", "m7.1", "m5.2", "f1",
    "f0", "f2", "f3", "f4", "v", "f6", "f7", "f5",
)
ODD_STEPS = (
    "c0", "c1", "p2", "p1", "p0", "a4", "w", "c2", "m1.1", "a5", "c3", "m0.1", "m1.2", "a6", "c4", "m2.1",
    "a7", "c5", "m0.2", "f1", "m3.1", "m4.1", "v", "f2", "m5.1", "f0", "f3", "f4", "f5",
)


def group_pairs(group):
    return sum(job[1] for job in group[1])


def group_phases(group):
    phases, chunks = [], SHARES
    for flips in group[0]:
        pieces = 2 ** len(flips)
        chunks //= pieces
        masks = [
            sum(FLIPS[name] for bit, name in enumerate(reversed(flips)) if piece >> bit & 1)
            for piece in range(pieces)
        ]
        phases.append((masks[1:], chunks))
    return phases


def group_order(group):
    names = "".join(group[0])[::-1]
    return [sum(FLIPS[name] for bit, name in enumerate(names) if at >> bit & 1) for at in range(SHARES)]


def packed(re, im):
    top = jnp.max(jnp.maximum(jnp.abs(re), jnp.abs(im)), axis=0, keepdims=True)
    power = jnp.ceil(jnp.log2(jnp.maximum(top, SMALLEST)))
    factor = FULL * jnp.exp2(-power)
    high = (re * factor + (MID + 0.5)).astype(jnp.int32)
    low = (im * factor + (MID + 0.5)).astype(jnp.int32)
    return lax.bitwise_or(lax.shift_left(high, jnp.full_like(high, 16)), low), power.astype(jnp.int32)


def unpacked(word, power):
    step = jnp.exp2(power.astype(jnp.float32)) * (1.0 / FULL)
    high = lax.shift_right_logical(word, jnp.full_like(word, 16)) - MID
    low = lax.bitwise_and(word, jnp.full_like(word, 65535)) - MID
    return high.astype(jnp.float32) * step, low.astype(jnp.float32) * step


class Plan:
    def __init__(self, groups, scratch, remote, peers):
        self.groups = groups
        self.acc, self.done, self.sent, self.got, self.sums = [], [], [], [], []
        rest = list(scratch)
        for group in groups:
            self.acc.append(rest.pop(0))
            self.done.append(rest.pop(0))
            self.sent.append([rest.pop(0) for _ in group[0]])
            self.got.append([rest.pop(0) for _ in group[0]])
            self.sums.append(
                [
                    [remote(sent.at[n], got.at[n], peers[mask]) for n, mask in enumerate(masks)]
                    for sent, got, (masks, _) in zip(self.sent[-1], self.got[-1], group_phases(group))
                ]
            )
        self.buffers = len(scratch) - len(rest)

    def exchange(self, remote, upper_ref, lower_ref, before, after):
        self.outgoing = []
        for group, done in zip(self.groups, self.done):
            total, s, copies = group_pairs(group), 0, []
            for column, pairs, row, offset in group[1]:
                for n in range(pairs):
                    if row - n < PREV:
                        at = (row - n + 1) * KOFF + offset + n
                        copies.append(remote(done.at[total + s + n], upper_ref.at[at], before))
                if column >= OWN:
                    at = (column - OWN) * KOFF + offset
                    copies.append(remote(done.at[pl.ds(s, pairs)], lower_ref.at[pl.ds(at, pairs)], after))
                s += pairs
            self.outgoing.append(copies)


class Guarded:
    def __init__(self, copy, sends, receives):
        self.copy, self.sends, self.receives = copy, sends, receives

    def start(self):
        pl.when(self.sends)(self.copy.start)

    def wait_send(self):
        pl.when(self.sends)(self.copy.wait_send)

    def wait_recv(self):
        pl.when(self.receives)(self.copy.wait_recv)


def kernel(reach_ref, valid_ref, gap_ref, spectra_ref, upper_ref, lower_ref, *scratch):
    staged, live, reach, valid, wide, left, turned, products, weights, weights_prev = scratch[:10]
    load_sem, send_sem, recv_sem = scratch[10:13]
    depth = spectra_ref.shape[0]
    half = depth // 2
    lanes = lax.axis_size("chan")
    chan = lax.axis_index("chan")
    freq = lax.axis_index("freq")
    x_own = freq // RING
    y_own = lax.rem(freq, RING)
    after = (lax.rem(chan + 1, lanes), freq)
    before = (lax.rem(chan + lanes - 1, lanes), freq)
    y_by_flips = [y_own, y_own + 1 - 2 * lax.rem(y_own, 2), RING - 1 - y_own, lax.rem(y_own + 2, RING)]
    places = [lax.rem(x_own + mask // RING, 2) * RING + y_by_flips[mask % RING] for mask in range(SHARES)]
    peers = [(chan, place) for place in places]
    has_after = chan < lanes - 1
    has_before = chan > 0

    barrier = pltpu.get_barrier_semaphore()
    for peer in [after, before] + peers[1:]:
        pl.semaphore_signal(barrier, inc=1, device_id=peer, device_id_type=ON_MESH)

    def column(b):
        return spectra_ref.at[:, pl.ds(b * LANE, LANE)]

    loads = [pltpu.make_async_copy(column(b), staged.at[b], load_sem.at[b]) for b in range(OWN)]
    loads.append(pltpu.make_async_copy(gap_ref, live.at[0], load_sem.at[OWN]))
    loads.append(pltpu.make_async_copy(reach_ref, reach, load_sem.at[OWN + 1]))
    loads.append(pltpu.make_async_copy(valid_ref, valid, load_sem.at[OWN + 2]))
    for copy in loads:
        copy.start()

    count = [0]

    def remote(source, target, peer):
        slot = count[0]
        count[0] = slot + 1
        copy = pltpu.make_async_remote_copy(
            src_ref=source,
            dst_ref=target,
            send_sem=send_sem.at[slot],
            recv_sem=recv_sem.at[slot],
            device_id=peer,
            device_id_type=ON_MESH,
        )
        if peer is after:
            return Guarded(copy, has_after, has_before)
        if peer is before:
            return Guarded(copy, has_before, has_after)
        return copy

    send_live = [remote(gap_ref, live.at[1], before), remote(gap_ref, live.at[2], after)]
    send_right = [remote(column(b), staged.at[OWN + b], before) for b in range(OWN)]
    send_left = [remote(column(b), staged.at[2 * OWN + b - 1], after) for b in range(1, OWN)]

    pl.semaphore_wait(barrier, 2 + len(peers) - 1)
    for copy in send_live + send_right + send_left[::-1]:
        copy.start()

    @pl.when(chan == lanes - 1)
    def _():
        live[1] = jnp.zeros_like(live[1])
        staged[OWN : 2 * OWN] = jnp.zeros_like(staged[OWN : 2 * OWN])
        for i in range(1, OWN):
            for k in range(KOFF - i, KOFF):
                upper_ref[i * KOFF + k] = jnp.zeros_like(upper_ref[0])

    @pl.when(chan == 0)
    def _():
        live[2] = jnp.zeros_like(live[2])
        staged[2 * OWN :] = jnp.zeros_like(staged[2 * OWN :])
        weights_prev[...] = jnp.zeros_like(weights_prev)
        for j in range(OWN):
            for k in range(j + 1, KOFF):
                lower_ref[j * KOFF + k] = jnp.zeros_like(lower_ref[0])

    def masked(slot, side, b):
        return staged[slot] * live[side, b : b + 1, :].astype(jnp.float32).astype(jnp.bfloat16)

    def widen(b, block):
        wide[b, :, :LANE] = block
        wide[b, :half, LANE:] = block[half:]
        wide[b, half:, LANE:] = -block[:half]

    def turn(row, block):
        for t in range(depth // LANE):
            turned[:, t * LANE : (t + 1) * LANE] = block[t * LANE : (t + 1) * LANE].T
        for mask in range(SHARES):
            at = pl.multiple_of(places[mask] * KEEP, KEEP)
            left[row, mask * KEEP : (mask + 1) * KEEP, :] = turned[pl.ds(at, KEEP), :]

    loads[OWN].wait()
    for b in range(OWN):
        loads[b].wait()
        block = masked(b, 0, b)
        widen(b, block)
        turn(PREV + b, block)

    send_weights = remote(weights, weights_prev, after)

    def weigh():
        loads[OWN + 1].wait()
        loads[OWN + 2].wait()
        for i in range(OWN):
            for k in range(KOFF):
                keep = (k < reach[i]) & (valid[i, k] > 0) & (chan * OWN + i + k < lanes * OWN)
                value = jnp.where(keep, 1.0 / math.sqrt(SEGS * BINS), 0.0).astype(jnp.float32)
                weights[i * KOFF + k : i * KOFF + k + 1, :] = jnp.full((1, LANE), value, jnp.float32)
        send_weights.start()

    def clear(plan, g, phase):
        total = group_pairs(plan.groups[g])
        masks, chunks = group_phases(plan.groups[g])[phase]
        for n in range(len(masks)):
            low, high = total * chunks * KEEP, plan.sent[g][phase].shape[1]
            plan.sent[g][phase][n, low:high, :] = jnp.zeros((high - low, LANE), jnp.int32)

    def put(ref, piece, rows, total, s, re, im):
        word, power = packed(re, im)
        ref[piece, pl.ds(pl.multiple_of(s * rows, rows), rows), :] = word
        at = pl.ds(total * rows + s // POWERS, 1)
        field = lax.shift_left(power + 128, jnp.full_like(power, 8 * lax.rem(s, POWERS)))
        ref[piece, at, :] = lax.bitwise_or(ref[piece, at, :], field)

    def take(ref, piece, rows, total, s):
        word = ref[piece, pl.ds(pl.multiple_of(s * rows, rows), rows), :]
        field = ref[piece, pl.ds(total * rows + s // POWERS, 1), :]
        field = lax.shift_right_logical(field, jnp.full_like(field, 8 * lax.rem(s, POWERS)))
        return unpacked(word, lax.bitwise_and(field, jnp.full_like(field, 255)) - 128)

    even = Plan(EVEN, scratch[13:], remote, peers)
    odd = Plan(ODD, scratch[13 + even.buffers :], remote, peers)
    even.exchange(remote, upper_ref, lower_ref, before, after)
    odd.exchange(remote, upper_ref, lower_ref, before, after)

    def run(plan, other, steps):
        def spread(g, phase, s, piece):
            total = group_pairs(plan.groups[g])
            masks, chunks = group_phases(plan.groups[g])[phase]
            rows = chunks * KEEP
            re, im = piece(0, chunks)
            plan.acc[g][s, 0, :rows] = re
            plan.acc[g][s, 1, :rows] = im
            for n in range(len(masks)):
                re, im = piece((n + 1) * chunks, (n + 2) * chunks)
                put(plan.sent[g][phase], n, rows, total, s, re, im)

        def gathered(g, phase, s):
            total = group_pairs(plan.groups[g])
            masks, chunks = group_phases(plan.groups[g])[phase]
            rows = chunks * KEEP
            re, im = plan.acc[g][s, 0, :rows], plan.acc[g][s, 1, :rows]
            for n in range(len(masks)):
                more_re, more_im = take(plan.got[g][phase], n, rows, total, s)
                re, im = re + more_re, im + more_im
            return re, im

        def compute(g):
            order = group_order(plan.groups[g])
            clear(plan, g, 0)
            base = 0
            for column, pairs, row, _ in plan.groups[g][1]:
                rows = left[row - pairs + 1 : row + 1].reshape(pairs * LANE, depth)
                products[: pairs * LANE] = jnp.dot(rows, wide[column], preferred_element_type=jnp.float32)

                def step(n, carry, pairs=pairs, base=base):
                    at = (pairs - 1 - n) * LANE

                    def piece(low, high):
                        parts = [
                            products[pl.ds(pl.multiple_of(at + order[p] * KEEP, KEEP), KEEP), :] for p in range(low, high)
                        ]
                        both = jnp.concatenate(parts, axis=0)
                        return both[:, :LANE], both[:, LANE:]

                    spread(g, 0, n + base, piece)
                    return carry

                lax.fori_loop(0, pairs, step, 0, unroll=True)
                base += pairs
            for copy in plan.sums[g][0]:
                copy.start()

        def middle(g, phase):
            clear(plan, g, phase)
            for copy in plan.sums[g][phase - 1]:
                copy.wait_recv()

            def step(s, carry):
                re, im = gathered(g, phase - 1, s)
                spread(g, phase, s, lambda low, high: (re[low * KEEP : high * KEEP], im[low * KEEP : high * KEEP]))
                return carry

            lax.fori_loop(0, group_pairs(plan.groups[g]), step, 0, unroll=True)
            for copy in plan.sums[g][phase]:
                copy.start()

        def finish(g):
            _, jobs = plan.groups[g]
            total = group_pairs(plan.groups[g])
            phase = len(plan.sums[g]) - 1
            for copy in plan.sums[g][phase]:
                copy.wait_recv()
            s = 0
            for column, pairs, row, offset in jobs:
                for n in range(pairs):
                    i, k = row - n - PREV, offset + n
                    re, im = gathered(g, phase, s)
                    at = (i % OWN) * KOFF + k
                    scale = (weights if i >= 0 else weights_prev)[at : at + 1, :]
                    re, im = re * scale, im * scale
                    if i >= 0:
                        upper_ref[at, 0] = re
                        upper_ref[at, 1] = im
                    if column < OWN:
                        lower_ref[column * KOFF + k, 0] = re
                        lower_ref[column * KOFF + k, 1] = -im
                    else:
                        plan.done[g][s, 0] = re
                        plan.done[g][s, 1] = -im
                    if i < 0:
                        plan.done[g][total + s, 0] = re
                        plan.done[g][total + s, 1] = im
                    s += 1
            for copy in plan.outgoing[g]:
                copy.start()

        def arrive(b):
            if b == OWN:
                send_live[0].wait_recv()
            send_right[b - OWN].wait_recv()
            widen(b, masked(b, 1, b - OWN))

        def precede(row):
            if row == PREV - 1:
                send_live[1].wait_recv()
            send_left[row].wait_recv()
            turn(row, masked(2 * OWN + row, 2, row + 1))

        for name in steps:
            numbers = [int(part) for part in name[1:].split(".") if part]
            {
                "a": arrive,
                "p": precede,
                "c": compute,
                "m": middle,
                "f": finish,
                "w": weigh,
                "v": send_weights.wait_recv,
            }[name[0]](*numbers)
        for group in other.outgoing:
            for copy in group:
                copy.wait_recv()
        for group in plan.outgoing:
            for copy in group:
                copy.wait_send()
        for group in plan.sums:
            for phase in group:
                for copy in phase:
                    copy.wait_send()

    @pl.when(lax.rem(chan, 2) == 0)
    def _():
        run(even, odd, EVEN_STEPS)

    @pl.when(lax.rem(chan, 2) == 1)
    def _():
        run(odd, even, ODD_STEPS)

    for copy in send_live + send_right + send_left + [send_weights]:
        copy.wait_send()


def scratch_shapes(depth):
    shapes = [
        pltpu.VMEM((2 * OWN + PREV, depth, LANE), jnp.bfloat16),
        pltpu.VMEM((3, OWN, LANE), jnp.int32),
        pltpu.SMEM((OWN,), jnp.int32),
        pltpu.SMEM((OWN, KOFF), jnp.int32),
        pltpu.VMEM((2 * OWN, depth, 2 * LANE), jnp.bfloat16),
        pltpu.VMEM((PREV + OWN, LANE, depth), jnp.bfloat16),
        pltpu.VMEM((LANE, depth), jnp.bfloat16),
        pltpu.VMEM(((OWN + PREV) * LANE, 2 * LANE), jnp.float32),
        pltpu.VMEM((OWN * KOFF, LANE), jnp.float32),
        pltpu.VMEM((OWN * KOFF, LANE), jnp.float32),
        pltpu.SemaphoreType.DMA((OWN + 3,)),
        pltpu.SemaphoreType.DMA((128,)),
        pltpu.SemaphoreType.DMA((128,)),
    ]
    for group in EVEN + ODD:
        total = group_pairs(group)
        phases = group_phases(group)
        moved = [
            pltpu.VMEM((len(masks), total * chunks * KEEP + pl.cdiv(total, POWERS), LANE), jnp.int32)
            for masks, chunks in phases
        ]
        shapes.append(pltpu.VMEM((total, 2, phases[0][1] * KEEP, LANE), jnp.float32))
        shapes.append(pltpu.VMEM((2 * total, 2, KEEP, LANE), jnp.float32))
        shapes += moved + moved
    return shapes


def shards(spectra, gap, reach, valid):
    depth = spectra.shape[0] * spectra.shape[1] * spectra.shape[2]
    flat = spectra.reshape(depth, spectra.shape[3])
    pairs = OWN * KOFF
    result = jax.ShapeDtypeStruct((pairs, 2, KEEP, LANE), jnp.float32)
    in_vmem = pl.BlockSpec(memory_space=pltpu.VMEM)
    anywhere = pl.BlockSpec(memory_space=pl.ANY)
    upper, lower = pl.pallas_call(
        kernel,
        out_shape=(result, result),
        in_specs=[anywhere] * 4,
        out_specs=(in_vmem, in_vmem),
        scratch_shapes=scratch_shapes(depth),
        compiler_params=pltpu.CompilerParams(
            collective_id=0, has_side_effects=True, vmem_limit_bytes=209 * 2**18
        ),
        cost_estimate=pl.CostEstimate(flops=4 * pairs * depth * LANE * LANE, bytes_accessed=2**21, transcendentals=0),
        name="spectral_pairs",
    )(*(pltpu.with_memory_space_constraint(a, pltpu.HBM) for a in (reach, valid, gap.reshape(OWN, LANE), flat)))
    order = (3, 0, 1, 2, 4)
    upper = upper.reshape(OWN, KOFF, 2, KEEP, LANE).transpose(order)
    lower = lower.reshape(OWN, KOFF, 2, KEEP, LANE).transpose(order)
    return upper, lower


def solution(mesh):
    placed = (P(None, None, "freq", "chan"), P("chan"), P("chan"), P("chan", None))
    return jax.shard_map(
        shards,
        mesh=mesh,
        in_specs=placed,
        out_specs=(P("freq", "chan", None, None, None), P("freq", "chan", None, None, None)),
        check_vma=False,
    )
```

```python
import math

import jax
import jax.numpy as jnp
from jax import lax
from jax.experimental import pallas as pl
from jax.experimental.pallas import tpu as pltpu
from jax.sharding import PartitionSpec as P

BINS = 2048
SEGS = 2
KOFF = 8
LANE = 128
OWN = 4
PREV = 3
KEEP = 16
RING = 4
SHARES = 8
POWERS = 4
FULL = 32700.0
MID = 32768
SMALLEST = 1e-33
ON_MESH = pl.DeviceIdType.MESH

FLIPS = {"x": 4, "b": 2, "a": 1}
OWN_FIRST = ((0, 1, 3, 0), (1, 2, 4, 0), (2, 3, 5, 0))
OWN_LAST = ((3, 4, 6, 0),)
EVEN = (
    (("b", "x", "a"), OWN_FIRST),
    (("a", "b", "x"), OWN_LAST),
    (("b", "a", "x"), ((4, 4, 6, 1),)),
    (("b", "x", "a"), ((5, 4, 6, 2),)),
    (("a", "b", "x"), ((6, 4, 6, 3),)),
    (("b", "a", "x"), ((7, 4, 6, 4),)),
    (("a", "x", "b"), ((4, 1, 2, 5), (5, 1, 2, 6), (6, 1, 2, 7))),
    (("b", "xa"), ((4, 2, 1, 6), (5, 1, 1, 7))),
)
ODD = (
    (("b", "a", "x"), OWN_FIRST),
    (("a", "x", "b"), OWN_LAST),
    (("a", "xb"), ((4, 7, 6, 1),)),
    (("x", "ab"), ((5, 6, 6, 2),)),
    (("a", "xb"), ((6, 5, 6, 3),)),
    (("xab",), ((7, 4, 6, 4),)),
)
EVEN_STEPS = (
    "c0", "c1", "a4", "w", "c2", "a5", "c3", "a6", "c4", "a7", "c5", "p2", "c6", "m1.1", "m0.1", "m4.1",
    "m2.1", "p1", "p0", "c7", "m3.1", "m6.1", "m5.1", "m0.2", "m1.2", "m2.2", "m4.2", "m3.2", "m6.2", "m7.1", "m5.2", "f1",
    "f0", "f2", "f3", "f4", "v", "f6", "f7", "f5",
)
ODD_STEPS = (
    "c0", "c1", "p2", "p1", "p0", "a4", "w", "c2", "m1.1", "a5", "c3", "m0.1", "m1.2", "a6", "c4", "m2.1",
    "a7", "c5", "m0.2", "f1", "m3.1", "m4.1", "v", "f2", "f0", "f3", "f4", "f5",
)


def group_pairs(group):
    return sum(job[1] for job in group[1])


def group_phases(group):
    phases, chunks = [], SHARES
    for flips in group[0]:
        pieces = 2 ** len(flips)
        chunks //= pieces
        masks = [
            sum(FLIPS[name] for bit, name in enumerate(reversed(flips)) if piece >> bit & 1)
            for piece in range(pieces)
        ]
        phases.append((masks[1:], chunks))
    return phases


def group_order(group):
    names = "".join(group[0])[::-1]
    return [sum(FLIPS[name] for bit, name in enumerate(names) if at >> bit & 1) for at in range(SHARES)]


def packed(re, im):
    top = jnp.max(jnp.maximum(jnp.abs(re), jnp.abs(im)), axis=0, keepdims=True)
    power = jnp.ceil(jnp.log2(jnp.maximum(top, SMALLEST)))
    factor = FULL * jnp.exp2(-power)
    high = (re * factor + (MID + 0.5)).astype(jnp.int32)
    low = (im * factor + (MID + 0.5)).astype(jnp.int32)
    return lax.bitwise_or(lax.shift_left(high, jnp.full_like(high, 16)), low), power.astype(jnp.int32)


def unpacked(word, power):
    step = jnp.exp2(power.astype(jnp.float32)) * (1.0 / FULL)
    high = lax.shift_right_logical(word, jnp.full_like(word, 16)) - MID
    low = lax.bitwise_and(word, jnp.full_like(word, 65535)) - MID
    return high.astype(jnp.float32) * step, low.astype(jnp.float32) * step


class Plan:
    def __init__(self, groups, scratch, remote, peers):
        self.groups = groups
        self.acc, self.done, self.sent, self.got, self.sums = [], [], [], [], []
        rest = list(scratch)
        for group in groups:
            self.acc.append(rest.pop(0))
            self.done.append(rest.pop(0))
            self.sent.append([rest.pop(0) for _ in group[0]])
            self.got.append([rest.pop(0) for _ in group[0]])
            self.sums.append(
                [
                    [remote(sent.at[n], got.at[n], peers[mask]) for n, mask in enumerate(masks)]
                    for sent, got, (masks, _) in zip(self.sent[-1], self.got[-1], group_phases(group))
                ]
            )
        self.buffers = len(scratch) - len(rest)

    def exchange(self, remote, upper_ref, lower_ref, before, after):
        self.outgoing = []
        for group, done in zip(self.groups, self.done):
            total, s, copies = group_pairs(group), 0, []
            for column, pairs, row, offset in group[1]:
                for n in range(pairs):
                    if row - n < PREV:
                        at = (row - n + 1) * KOFF + offset + n
                        copies.append(remote(done.at[total + s + n], upper_ref.at[at], before))
                if column >= OWN:
                    at = (column - OWN) * KOFF + offset
                    copies.append(remote(done.at[pl.ds(s, pairs)], lower_ref.at[pl.ds(at, pairs)], after))
                s += pairs
            self.outgoing.append(copies)


class Guarded:
    def __init__(self, copy, sends, receives):
        self.copy, self.sends, self.receives = copy, sends, receives

    def start(self):
        pl.when(self.sends)(self.copy.start)

    def wait_send(self):
        pl.when(self.sends)(self.copy.wait_send)

    def wait_recv(self):
        pl.when(self.receives)(self.copy.wait_recv)


def kernel(reach_ref, valid_ref, gap_ref, spectra_ref, upper_ref, lower_ref, *scratch):
    staged, live, reach, valid, wide, left, turned, products, weights, weights_prev = scratch[:10]
    load_sem, send_sem, recv_sem = scratch[10:13]
    depth = spectra_ref.shape[0]
    half = depth // 2
    lanes = lax.axis_size("chan")
    chan = lax.axis_index("chan")
    freq = lax.axis_index("freq")
    x_own = freq // RING
    y_own = lax.rem(freq, RING)
    after = (lax.rem(chan + 1, lanes), freq)
    before = (lax.rem(chan + lanes - 1, lanes), freq)
    y_by_flips = [y_own, y_own + 1 - 2 * lax.rem(y_own, 2), RING - 1 - y_own, lax.rem(y_own + 2, RING)]
    places = [lax.rem(x_own + mask // RING, 2) * RING + y_by_flips[mask % RING] for mask in range(SHARES)]
    peers = [(chan, place) for place in places]
    has_after = chan < lanes - 1
    has_before = chan > 0

    barrier = pltpu.get_barrier_semaphore()
    for peer in [after, before] + peers[1:]:
        pl.semaphore_signal(barrier, inc=1, device_id=peer, device_id_type=ON_MESH)

    def column(b):
        return spectra_ref.at[:, pl.ds(b * LANE, LANE)]

    loads = [pltpu.make_async_copy(column(b), staged.at[b], load_sem.at[b]) for b in range(OWN)]
    loads.append(pltpu.make_async_copy(gap_ref, live.at[0], load_sem.at[OWN]))
    loads.append(pltpu.make_async_copy(reach_ref, reach, load_sem.at[OWN + 1]))
    loads.append(pltpu.make_async_copy(valid_ref, valid, load_sem.at[OWN + 2]))
    for copy in loads:
        copy.start()

    count = [0]

    def remote(source, target, peer):
        slot = count[0]
        count[0] = slot + 1
        copy = pltpu.make_async_remote_copy(
            src_ref=source,
            dst_ref=target,
            send_sem=send_sem.at[slot],
            recv_sem=recv_sem.at[slot],
            device_id=peer,
            device_id_type=ON_MESH,
        )
        if peer is after:
            return Guarded(copy, has_after, has_before)
        if peer is before:
            return Guarded(copy, has_before, has_after)
        return copy

    send_live = [remote(gap_ref, live.at[1], before), remote(gap_ref, live.at[2], after)]
    send_right = [remote(column(b), staged.at[OWN + b], before) for b in range(OWN)]
    send_left = [remote(column(b), staged.at[2 * OWN + b - 1], after) for b in range(1, OWN)]

    @pl.when(chan == lanes - 1)
    def _():
        live[1] = jnp.zeros_like(live[1])
        staged[OWN : 2 * OWN] = jnp.zeros_like(staged[OWN : 2 * OWN])
        for i in range(1, OWN):
            for k in range(KOFF - i, KOFF):
                upper_ref[i * KOFF + k] = jnp.zeros_like(upper_ref[0])

    @pl.when(chan == 0)
    def _():
        live[2] = jnp.zeros_like(live[2])
        staged[2 * OWN :] = jnp.zeros_like(staged[2 * OWN :])
        weights_prev[...] = jnp.zeros_like(weights_prev)
        for j in range(OWN):
            for k in range(j + 1, KOFF):
                lower_ref[j * KOFF + k] = jnp.zeros_like(lower_ref[0])

    def masked(slot, side, b):
        return staged[slot] * live[side, b : b + 1, :].astype(jnp.float32).astype(jnp.bfloat16)

    def widen(b, block):
        wide[b, :, :LANE] = block
        wide[b, :half, LANE:] = block[half:]
        wide[b, half:, LANE:] = -block[:half]

    def turn(row, block):
        for t in range(depth // LANE):
            turned[:, t * LANE : (t + 1) * LANE] = block[t * LANE : (t + 1) * LANE].T
        for mask in range(SHARES):
            at = pl.multiple_of(places[mask] * KEEP, KEEP)
            left[row, mask * KEEP : (mask + 1) * KEEP, :] = turned[pl.ds(at, KEEP), :]

    loads[OWN].wait()
    for b in range(OWN):
        loads[b].wait()
        block = masked(b, 0, b)
        widen(b, block)
        turn(PREV + b, block)

    pl.semaphore_wait(barrier, 2 + len(peers) - 1)
    for copy in send_live + send_right + send_left[::-1]:
        copy.start()

    send_weights = remote(weights, weights_prev, after)

    def weigh():
        loads[OWN + 1].wait()
        loads[OWN + 2].wait()
        for i in range(OWN):
            for k in range(KOFF):
                keep = (k < reach[i]) & (valid[i, k] > 0) & (chan * OWN + i + k < lanes * OWN)
                value = jnp.where(keep, 1.0 / math.sqrt(SEGS * BINS), 0.0).astype(jnp.float32)
                weights[i * KOFF + k : i * KOFF + k + 1, :] = jnp.full((1, LANE), value, jnp.float32)
        send_weights.start()

    def clear(plan, g, phase):
        total = group_pairs(plan.groups[g])
        masks, chunks = group_phases(plan.groups[g])[phase]
        for n in range(len(masks)):
            low, high = total * chunks * KEEP, plan.sent[g][phase].shape[1]
            plan.sent[g][phase][n, low:high, :] = jnp.zeros((high - low, LANE), jnp.int32)

    def put(ref, piece, rows, total, s, re, im):
        word, power = packed(re, im)
        ref[piece, pl.ds(pl.multiple_of(s * rows, rows), rows), :] = word
        at = pl.ds(total * rows + s // POWERS, 1)
        field = lax.shift_left(power + 128, jnp.full_like(power, 8 * lax.rem(s, POWERS)))
        ref[piece, at, :] = lax.bitwise_or(ref[piece, at, :], field)

    def take(ref, piece, rows, total, s):
        word = ref[piece, pl.ds(pl.multiple_of(s * rows, rows), rows), :]
        field = ref[piece, pl.ds(total * rows + s // POWERS, 1), :]
        field = lax.shift_right_logical(field, jnp.full_like(field, 8 * lax.rem(s, POWERS)))
        return unpacked(word, lax.bitwise_and(field, jnp.full_like(field, 255)) - 128)

    even = Plan(EVEN, scratch[13:], remote, peers)
    odd = Plan(ODD, scratch[13 + even.buffers :], remote, peers)
    even.exchange(remote, upper_ref, lower_ref, before, after)
    odd.exchange(remote, upper_ref, lower_ref, before, after)

    def run(plan, other, steps):
        def spread(g, phase, s, piece):
            total = group_pairs(plan.groups[g])
            masks, chunks = group_phases(plan.groups[g])[phase]
            rows = chunks * KEEP
            re, im = piece(0, chunks)
            plan.acc[g][s, 0, :rows] = re
            plan.acc[g][s, 1, :rows] = im
            for n in range(len(masks)):
                re, im = piece((n + 1) * chunks, (n + 2) * chunks)
                put(plan.sent[g][phase], n, rows, total, s, re, im)

        def gathered(g, phase, s):
            total = group_pairs(plan.groups[g])
            masks, chunks = group_phases(plan.groups[g])[phase]
            rows = chunks * KEEP
            re, im = plan.acc[g][s, 0, :rows], plan.acc[g][s, 1, :rows]
            for n in range(len(masks)):
                more_re, more_im = take(plan.got[g][phase], n, rows, total, s)
                re, im = re + more_re, im + more_im
            return re, im

        def compute(g):
            order = group_order(plan.groups[g])
            clear(plan, g, 0)
            base = 0
            for column, pairs, row, _ in plan.groups[g][1]:
                rows = left[row - pairs + 1 : row + 1].reshape(pairs * LANE, depth)
                products[: pairs * LANE] = jnp.dot(rows, wide[column], preferred_element_type=jnp.float32)

                def step(n, carry, pairs=pairs, base=base):
                    at = (pairs - 1 - n) * LANE

                    def piece(low, high):
                        parts = [
                            products[pl.ds(pl.multiple_of(at + order[p] * KEEP, KEEP), KEEP), :] for p in range(low, high)
                        ]
                        both = jnp.concatenate(parts, axis=0)
                        return both[:, :LANE], both[:, LANE:]

                    spread(g, 0, n + base, piece)
                    return carry

                lax.fori_loop(0, pairs, step, 0, unroll=True)
                base += pairs
            for copy in plan.sums[g][0]:
                copy.start()

        def middle(g, phase):
            clear(plan, g, phase)
            for copy in plan.sums[g][phase - 1]:
                copy.wait_recv()

            def step(s, carry):
                re, im = gathered(g, phase - 1, s)
                spread(g, phase, s, lambda low, high: (re[low * KEEP : high * KEEP], im[low * KEEP : high * KEEP]))
                return carry

            lax.fori_loop(0, group_pairs(plan.groups[g]), step, 0, unroll=True)
            for copy in plan.sums[g][phase]:
                copy.start()

        def finish(g):
            _, jobs = plan.groups[g]
            total = group_pairs(plan.groups[g])
            phase = len(plan.sums[g]) - 1
            for copy in plan.sums[g][phase]:
                copy.wait_recv()
            s = 0
            for column, pairs, row, offset in jobs:
                for n in range(pairs):
                    i, k = row - n - PREV, offset + n
                    re, im = gathered(g, phase, s)
                    at = (i % OWN) * KOFF + k
                    scale = (weights if i >= 0 else weights_prev)[at : at + 1, :]
                    re, im = re * scale, im * scale
                    if i >= 0:
                        upper_ref[at, 0] = re
                        upper_ref[at, 1] = im
                    if column < OWN:
                        lower_ref[column * KOFF + k, 0] = re
                        lower_ref[column * KOFF + k, 1] = -im
                    else:
                        plan.done[g][s, 0] = re
                        plan.done[g][s, 1] = -im
                    if i < 0:
                        plan.done[g][total + s, 0] = re
                        plan.done[g][total + s, 1] = im
                    s += 1
            for copy in plan.outgoing[g]:
                copy.start()

        def arrive(b):
            if b == OWN:
                send_live[0].wait_recv()
            send_right[b - OWN].wait_recv()
            widen(b, masked(b, 1, b - OWN))

        def precede(row):
            if row == PREV - 1:
                send_live[1].wait_recv()
            send_left[row].wait_recv()
            turn(row, masked(2 * OWN + row, 2, row + 1))

        for name in steps:
            numbers = [int(part) for part in name[1:].split(".") if part]
            {
                "a": arrive,
                "p": precede,
                "c": compute,
                "m": middle,
                "f": finish,
                "w": weigh,
                "v": send_weights.wait_recv,
            }[name[0]](*numbers)
        for group in other.outgoing:
            for copy in group:
                copy.wait_recv()
        for group in plan.outgoing:
            for copy in group:
                copy.wait_send()
        for group in plan.sums:
            for phase in group:
                for copy in phase:
                    copy.wait_send()

    @pl.when(lax.rem(chan, 2) == 0)
    def _():
        run(even, odd, EVEN_STEPS)

    @pl.when(lax.rem(chan, 2) == 1)
    def _():
        run(odd, even, ODD_STEPS)

    for copy in send_live + send_right + send_left + [send_weights]:
        copy.wait_send()


def scratch_shapes(depth):
    shapes = [
        pltpu.VMEM((2 * OWN + PREV, depth, LANE), jnp.bfloat16),
        pltpu.VMEM((3, OWN, LANE), jnp.int32),
        pltpu.SMEM((OWN,), jnp.int32),
        pltpu.SMEM((OWN, KOFF), jnp.int32),
        pltpu.VMEM((2 * OWN, depth, 2 * LANE), jnp.bfloat16),
        pltpu.VMEM((PREV + OWN, LANE, depth), jnp.bfloat16),
        pltpu.VMEM((LANE, depth), jnp.bfloat16),
        pltpu.VMEM(((OWN + PREV) * LANE, 2 * LANE), jnp.float32),
        pltpu.VMEM((OWN * KOFF, LANE), jnp.float32),
        pltpu.VMEM((OWN * KOFF, LANE), jnp.float32),
        pltpu.SemaphoreType.DMA((OWN + 3,)),
        pltpu.SemaphoreType.DMA((128,)),
        pltpu.SemaphoreType.DMA((128,)),
    ]
    for group in EVEN + ODD:
        total = group_pairs(group)
        phases = group_phases(group)
        moved = [
            pltpu.VMEM((len(masks), total * chunks * KEEP + pl.cdiv(total, POWERS), LANE), jnp.int32)
            for masks, chunks in phases
        ]
        shapes.append(pltpu.VMEM((total, 2, phases[0][1] * KEEP, LANE), jnp.float32))
        shapes.append(pltpu.VMEM((2 * total, 2, KEEP, LANE), jnp.float32))
        shapes += moved + moved
    return shapes


def shards(spectra, gap, reach, valid):
    depth = spectra.shape[0] * spectra.shape[1] * spectra.shape[2]
    flat = spectra.reshape(depth, spectra.shape[3])
    pairs = OWN * KOFF
    result = jax.ShapeDtypeStruct((pairs, 2, KEEP, LANE), jnp.float32)
    in_vmem = pl.BlockSpec(memory_space=pltpu.VMEM)
    anywhere = pl.BlockSpec(memory_space=pl.ANY)
    upper, lower = pl.pallas_call(
        kernel,
        out_shape=(result, result),
        in_specs=[anywhere] * 4,
        out_specs=(in_vmem, in_vmem),
        scratch_shapes=scratch_shapes(depth),
        compiler_params=pltpu.CompilerParams(
            collective_id=0, has_side_effects=True, vmem_limit_bytes=209 * 2**18
        ),
        cost_estimate=pl.CostEstimate(flops=4 * pairs * depth * LANE * LANE, bytes_accessed=2**21, transcendentals=0),
        name="spectral_pairs",
    )(*(pltpu.with_memory_space_constraint(a, pltpu.HBM) for a in (reach, valid, gap.reshape(OWN, LANE), flat)))
    order = (3, 0, 1, 2, 4)
    upper = upper.reshape(OWN, KOFF, 2, KEEP, LANE).transpose(order)
    lower = lower.reshape(OWN, KOFF, 2, KEEP, LANE).transpose(order)
    return upper, lower


def solution(mesh):
    placed = (P(None, None, "freq", "chan"), P("chan"), P("chan"), P("chan", None))
    return jax.shard_map(
        shards,
        mesh=mesh,
        in_specs=placed,
        out_specs=(P("freq", "chan", None, None, None), P("freq", "chan", None, None, None)),
        check_vma=False,
    )
```
